32 devices in a mesh: gx: 4 (over y, core), gy: 8 (over z, x).
Axes of the slice: x: 2, y: 2, z: 4, core: 2. Of those that a mesh axis runs over, the one named last changes fastest.
Arguments:
- conserved: float32 [5, 1, 1536, 1024], P(None, None, 'gx', 'gy'), may hold values from -0.375 to 3.33, as said below
- time_step: float32 [1, 1536, 1024], P(None, 'gx', 'gy'), may hold values from 200 to 1600
Outputs:
- update: float32 [5, 1, 1536, 1024], P(None, None, 'gx', 'gy')
The draws below stay inside these ranges and needn't reach their ends.
Inputs may be any that keep to these rules, and one draw needn't show every extreme that they name: conserved holds the conserved variables of a gas with heat ratio 1.4; density and pressure lie within 0.8 to 1.25 and each velocity component within -0.3 to 0.3.
All inputs are finite; a program needn't handle non-finite values.
Results may differ from the reference program's by a relative error of at most 0.0003.
Values sent between devices are 32-bit elements; how exact they have to be, the bound alone decides.
A program may use at most 128 MiB of HBM per device.

```python
import math
import jax
import jax.numpy as jnp
from jax import lax

NZ = 1
NX = 1536
NY = 1024


def draw_conserved(key, part):
    keys = jax.random.split(key, 5)
    shape = (NZ, NX, NY)
    pressure = jnp.exp(jax.random.uniform(keys[1], shape, jnp.float32, math.log(0.8), math.log(1.25)))
    density = jnp.exp(jax.random.uniform(keys[0], shape, jnp.float32, math.log(0.8), math.log(1.25)))
    vel_x = jax.random.uniform(keys[2], shape, jnp.float32, -0.3, 0.3)
    vel_y = jax.random.uniform(keys[3], shape, jnp.float32, -0.3, 0.3)
    vel_z = jax.random.uniform(keys[4], shape, jnp.float32, -0.3, 0.3)
    energy = pressure / 0.4 + 0.5 * density * (vel_x * vel_x + vel_y * vel_y + vel_z * vel_z)
    return jnp.stack([density, density * vel_x, density * vel_y, density * vel_z, energy])


def block_levels(own_key, extent, shards, smallest, largest):
    loudness = 1.0
    for axis_at, parts in shards:
        steps = jax.random.uniform(jax.random.fold_in(jax.random.fold_in(own_key, 6), axis_at), (parts,), jnp.float32, smallest / len(shards), largest / len(shards))
        loudness = loudness * jnp.repeat(jnp.exp(steps), extent[axis_at] // parts).reshape((-1,) + (1,) * (len(extent) - 1 - axis_at))
    return loudness


def setup_inputs(seed: int = 0) -> dict:
    streams_of = jax.random.split(jax.random.key(seed), 3)
    return {
        "conserved": draw_conserved(jax.random.fold_in(streams_of[2], 71), 0),
        "time_step": jnp.clip(jnp.exp(math.log(1600.0) - 2.0794415 * jax.random.uniform(streams_of[1], (NZ, NX, NY), jnp.float32) ** block_levels(streams_of[1], (NZ, NX, NY), ((1, 4), (2, 8)), -0.2, 0.2)), 200.0, 1600.0),
    }


HEAT_RATIO = 1.4
EPS_EXPLICIT = 0.02
EPS_IMPLICIT = 0.125

def primitive(conserved, density):
    vel_x = conserved[1] / density
    vel_y = conserved[2] / density
    vel_z = conserved[3] / density
    pressure = (HEAT_RATIO - 1.0) * (conserved[4] - 0.5 * (conserved[1] * vel_x + conserved[2] * vel_y + conserved[3] * vel_z))
    sound_sq = HEAT_RATIO * pressure / density
    return (vel_x, vel_y, vel_z, pressure, sound_sq)

def fluxes(conserved, density):
    vel_x, vel_y, vel_z, pressure, sound_sq = primitive(conserved, density)
    enthalpy_flow = conserved[4] + pressure
    flux_x = jnp.stack([conserved[1], conserved[1] * vel_x + pressure, conserved[2] * vel_x, conserved[3] * vel_x, enthalpy_flow * vel_x])
    flux_y = jnp.stack([conserved[2], conserved[1] * vel_y, conserved[2] * vel_y + pressure, conserved[3] * vel_y, enthalpy_flow * vel_y])
    return (flux_x, flux_y)

def central_x(padded):
    inner = padded[..., 2:-2]
    return (inner[..., 0:-4, :] - 8.0 * inner[..., 1:-3, :] + 8.0 * inner[..., 3:-1, :] - inner[..., 4:, :]) / 12.0

def central_y(padded):
    inner = padded[..., 2:-2, :]
    return (inner[..., 0:-4] - 8.0 * inner[..., 1:-3] + 8.0 * inner[..., 3:-1] - inner[..., 4:]) / 12.0

def fourth_x(padded):
    inner = padded[..., 2:-2]
    return inner[..., 0:-4, :] - 4.0 * inner[..., 1:-3, :] + 6.0 * inner[..., 2:-2, :] - 4.0 * inner[..., 3:-1, :] + inner[..., 4:, :]

def fourth_y(padded):
    inner = padded[..., 2:-2, :]
    return inner[..., 0:-4] - 4.0 * inner[..., 1:-3] + 6.0 * inner[..., 2:-2] - 4.0 * inner[..., 3:-1] + inner[..., 4:]

def residual_of(state_pad, flux_x_pad, flux_y_pad):
    return -(central_x(flux_x_pad) + central_y(flux_y_pad) + EPS_EXPLICIT * (fourth_x(state_pad) + fourth_y(state_pad)))

def wave_speeds(conserved, density):
    vel_x, vel_y, vel_z, pressure, sound_sq = primitive(conserved, density)
    sound = jnp.sqrt(sound_sq)
    return jnp.stack([vel_x, vel_x, vel_x, vel_x + sound, vel_x - sound])

def to_waves(conserved, residual):
    vel_x, vel_y, vel_z, pressure, sound_sq = primitive(conserved, conserved[0])
    sound = jnp.sqrt(sound_sq)
    factor = HEAT_RATIO - 1.0
    speed_sq = vel_x * vel_x + vel_y * vel_y + vel_z * vel_z
    moment = vel_x * residual[1] + vel_y * residual[2] + vel_z * residual[3]
    entropy = (1.0 - factor * speed_sq / (2.0 * sound_sq)) * residual[0] + factor / sound_sq * (moment - residual[4])
    common = factor / (2.0 * sound_sq) * (0.5 * speed_sq * residual[0] - moment + residual[4])
    acoustic = (residual[1] - vel_x * residual[0]) / (2.0 * sound)
    return jnp.stack([entropy, residual[2] - vel_y * residual[0], residual[3] - vel_z * residual[0], common + acoustic, common - acoustic])

def from_waves(conserved, waves):
    vel_x, vel_y, vel_z, pressure, sound_sq = primitive(conserved, conserved[0])
    sound = jnp.sqrt(sound_sq)
    speed_sq = vel_x * vel_x + vel_y * vel_y + vel_z * vel_z
    enthalpy = sound_sq / (HEAT_RATIO - 1.0) + 0.5 * speed_sq
    acoustic_sum = waves[3] + waves[4]
    return jnp.stack([waves[0] + acoustic_sum, vel_x * waves[0] + (vel_x + sound) * waves[3] + (vel_x - sound) * waves[4], vel_y * waves[0] + waves[1] + vel_y * acoustic_sum, vel_z * waves[0] + waves[2] + vel_z * acoustic_sum, 0.5 * speed_sq * waves[0] + vel_y * waves[1] + vel_z * waves[2] + (enthalpy + vel_x * sound) * waves[3] + (enthalpy - vel_x * sound) * waves[4]])

def band(speeds_padded, time_step):
    centre = speeds_padded[:, :, 1:-1]
    upper_face = 0.5 * (centre + speeds_padded[:, :, 2:])
    lower_face = 0.5 * (speeds_padded[:, :, :-2] + centre)
    lower_one = -0.5 * lower_face - 4.0 * EPS_IMPLICIT
    diagonal = jnp.broadcast_to(1.0 / time_step + 6.0 * EPS_IMPLICIT, centre.shape)
    upper_one = 0.5 * upper_face - 4.0 * EPS_IMPLICIT
    return (lower_one, diagonal, upper_one)

def solve_lines(lower_one, diagonal, upper_one, right_side):
    zero_row = jnp.zeros(right_side.shape[1:], jnp.float32)

    def forward(carried, row_data):
        prev_p, prev_q, prev_g, last_p, last_q, last_g = carried
        low_row, mid_row, upp_row, rhs_row = row_data
        reduced_low = low_row - EPS_IMPLICIT * prev_p
        pivot_value = mid_row - EPS_IMPLICIT * prev_q - reduced_low * last_p
        new_p = (upp_row - reduced_low * last_q) / pivot_value
        new_q = EPS_IMPLICIT / pivot_value
        new_g = (rhs_row - EPS_IMPLICIT * prev_g - reduced_low * last_g) / pivot_value
        return ((last_p, last_q, last_g, new_p, new_q, new_g), (new_p, new_q, new_g))
    start = (zero_row, zero_row, zero_row, zero_row, zero_row, zero_row)
    _, (coef_p, coef_q, coef_g) = lax.scan(forward, start, (lower_one, diagonal, upper_one, right_side))

    def backward(carried, row_data):
        next_one, next_two = carried
        new_p, new_q, new_g = row_data
        value_now = new_g - new_p * next_one - new_q * next_two
        return ((value_now, next_one), value_now)
    _, solution = lax.scan(backward, (zero_row, zero_row), (coef_p, coef_q, coef_g), reverse=True)
    return solution

def reference(conserved, time_step):
    flux_x, flux_y = fluxes(conserved, conserved[0])
    widths = ((0, 0), (0, 0), (2, 2), (2, 2))
    residual = residual_of(jnp.pad(conserved, widths), jnp.pad(flux_x, widths), jnp.pad(flux_y, widths))
    waves = to_waves(conserved, residual)
    speeds = wave_speeds(conserved, conserved[0])
    speeds_padded = jnp.pad(speeds, ((0, 0), (0, 0), (1, 1), (0, 0)), mode='edge')
    lower_one, diagonal, upper_one = band(speeds_padded, time_step)
    columns = []
    for field_no in range(5):
        solution = solve_lines(jnp.moveaxis(lower_one[field_no], 1, 0), jnp.moveaxis(diagonal[field_no], 1, 0), jnp.moveaxis(upper_one[field_no], 1, 0), jnp.moveaxis(waves[field_no], 1, 0))
        columns.append(jnp.moveaxis(solution, 0, 1))
    solved = jnp.stack(columns)
    return from_waves(conserved, solved)
```

```python
import functools
import jax
import jax.numpy as jnp
from jax import lax
from jax.experimental import pallas as pl
from jax.experimental.pallas import tpu as pltpu
from jax.sharding import PartitionSpec as P

EPS = 0.02
MESH = pl.DeviceIdType.MESH
ROWS_PACK = 72
FAMILY = (0, 0, 0, 1, 2)


def primitive(q):
    inv = 1.0 / q[0]
    u = q[1] * inv
    v = q[2] * inv
    w = q[3] * inv
    p = 0.4 * (q[4] - 0.5 * (q[1] * u + q[2] * v + q[3] * w))
    c2 = 1.4 * p * inv
    return u, v, w, p, c2


def flux_x(q, u, p):
    return [q[1], q[1] * u + p, q[2] * u, q[3] * u, (q[4] + p) * u]


def flux_y(q, v, p):
    return [q[2], q[1] * v, q[2] * v + p, q[3] * v, (q[4] + p) * v]


def mm(a, b):
    return (
        a[0] * b[0] + a[1] * b[2],
        a[0] * b[1] + a[1] * b[3],
        a[2] * b[0] + a[3] * b[2],
        a[2] * b[1] + a[3] * b[3],
    )


def mv(a, x):
    return (a[0] * x[0] + a[1] * x[1], a[2] * x[0] + a[3] * x[1])


def add(a, b):
    return tuple(x + y for x, y in zip(a, b))


def schur_inverse(x, y):
    pr = mm(y, x)
    m0, m1, m2, m3 = 1.0 - pr[0], -pr[1], -pr[2], 1.0 - pr[3]
    r = 1.0 / (m0 * m3 - m1 * m2)
    return (m3 * r, -m1 * r, -m2 * r, m0 * r)


def merge(mats_a, mats_b, rhs_a, rhs_b, last=False):
    mats, rec_m, invs = [], [], []
    for (hl_a, hr_a, tl_a, tr_a), (hl_b, hr_b, tl_b, tr_b) in zip(mats_a, mats_b):
        minv = schur_inverse(tr_a, hl_b)
        invs.append(minv)
        if last:
            continue
        head_l = mm(minv, mm(hl_b, tl_a))
        head_r = mm(minv, hr_b)
        tail_l = add(tl_a, mm(tr_a, head_l))
        tail_r = mm(tr_a, head_r)
        mats.append(
            (
                add(hl_a, mm(hr_a, head_l)),
                mm(hr_a, head_r),
                mm(tl_b, tail_l),
                add(tr_b, mm(tl_b, tail_r)),
            )
        )
        rec_m.append((head_l, head_r, tail_l, tail_r))
    rhs, rec_y = [], []
    for f, ((h_a, t_a), (h_b, t_b)) in enumerate(zip(rhs_a, rhs_b)):
        m = FAMILY[f]
        hl_b, tr_a = mats_b[m][0], mats_a[m][3]
        head_y = mv(invs[m], add(h_b, mv(hl_b, t_a)))
        tail_y = add(t_a, mv(tr_a, head_y))
        rec_y.append((head_y, tail_y))
        if not last:
            rhs.append((add(h_a, mv(mats_a[m][1], head_y)), add(t_b, mv(mats_b[m][2], tail_y))))
    return mats, rhs, (rec_m, rec_y)


def shifted(tree, d):
    return jax.tree.map(lambda x: pltpu.roll(x, 8 - d, 0), tree)


def reduce_levels(mats, rhs, strides, root):
    records = []
    for d in strides:
        last = root and d == strides[-1]
        mats, rhs, rec = merge(mats, shifted(mats, d), rhs, shifted(rhs, d), last)
        records.append(rec)
    return mats, rhs, records


def expand_levels(records, strides, left, right, sub, root):
    for d, (rec_m, rec_y) in reversed(list(zip(strides, records))):
        upper = (sub & d) != 0
        for f in range(5):
            head, tail = rec_y[f]
            if left[f] is not None:
                hl, hr, tl, tr = rec_m[FAMILY[f]]
                head = add(add(head, mv(hl, left[f])), mv(hr, right[f]))
                tail = add(add(tail, mv(tl, left[f])), mv(tr, right[f]))
                lo, hi = left[f], right[f]
            else:
                lo = hi = (jnp.zeros_like(head[0]),) * 2
            left[f] = tuple(jnp.where(upper, pltpu.roll(x, d, 0), y) for x, y in zip(tail, lo))
            right[f] = tuple(jnp.where(upper, pltpu.roll(y, d, 0), x) for x, y in zip(head, hi))
    return left, right


def kernel(
    nx, ny, rows,
    q_hbm, dt_hbm, out_hbm,
    qin, dtin, oout, hl, hr, eqs, fs, us, vs, ws, cs, rcs, res, mat, gs,
    wsend, wl, wr, pack, gath,
    in_sem, out_sem, hx_send, hx_recv, wy_send, wy_recv, g_send, g_recv,
):
    T = rows // 8
    ix = lax.axis_index("gx")
    iy = lax.axis_index("gy")
    has_l, has_r = ix > 0, ix < nx - 1
    has_d, has_u = iy > 0, iy < ny - 1
    cp_q = pltpu.make_async_copy(q_hbm, qin, in_sem.at[0])
    cp_t = pltpu.make_async_copy(dt_hbm, dtin, in_sem.at[1])
    cp_q.start()
    cp_t.start()

    barrier = pltpu.get_barrier_semaphore()
    for d in range(1, nx):
        pl.semaphore_signal(barrier, inc=1, device_id=(lax.rem(ix + d, nx), iy), device_id_type=MESH)

    @pl.when(has_d)
    def _():
        pl.semaphore_signal(barrier, inc=1, device_id=(ix, iy - 1), device_id_type=MESH)

    @pl.when(has_u)
    def _():
        pl.semaphore_signal(barrier, inc=1, device_id=(ix, iy + 1), device_id_type=MESH)

    def remote(src, dst, s_sem, r_sem, target):
        return pltpu.make_async_remote_copy(
            src_ref=src, dst_ref=dst, send_sem=s_sem, recv_sem=r_sem,
            device_id=target, device_id_type=MESH,
        )

    right_x = (lax.rem(ix + 1, nx), iy)
    left_x = (lax.rem(ix + nx - 1, nx), iy)
    up_y = (ix, lax.rem(iy + 1, ny))
    down_y = (ix, lax.rem(iy + ny - 1, ny))
    hx_to_r = remote(q_hbm.at[:, pl.ds(rows - 8, 8), :], hl, hx_send.at[0], hx_recv.at[0], right_x)
    hx_to_l = remote(q_hbm.at[:, pl.ds(0, 8), :], hr, hx_send.at[1], hx_recv.at[1], left_x)
    w_to_u = remote(wsend, wl, wy_send.at[0], wy_recv.at[0], up_y)
    w_to_d = remote(wsend, wr, wy_send.at[1], wy_recv.at[1], down_y)

    if ny > 1:
        both = jnp.logical_and(has_d, has_u)

        @pl.when(both)
        def _():
            pl.semaphore_wait(barrier, nx + 1)

        @pl.when(jnp.logical_not(both))
        def _():
            pl.semaphore_wait(barrier, nx)
    else:
        pl.semaphore_wait(barrier, nx - 1)

    pl.when(has_r)(hx_to_r.start)
    pl.when(has_l)(hx_to_l.start)

    @pl.when(jnp.logical_not(has_l))
    def _():
        hl[...] = jnp.zeros_like(hl)

    @pl.when(jnp.logical_not(has_r))
    def _():
        hr[...] = jnp.zeros_like(hr)

    @pl.when(jnp.logical_not(has_d))
    def _():
        wl[...] = jnp.zeros_like(wl)

    @pl.when(jnp.logical_not(has_u))
    def _():
        wr[...] = jnp.zeros_like(wr)

    if nx < 8:
        gath[pl.ds(nx * ROWS_PACK, (8 - nx) * ROWS_PACK), :] = jnp.zeros(
            ((8 - nx) * ROWS_PACK, 128), jnp.float32
        )

    shape = (8, 128)
    lane = lax.broadcasted_iota(jnp.int32, shape, 1)
    sub = lax.broadcasted_iota(jnp.int32, shape, 0)
    zero = jnp.where(lane + sub < 0, 1.0, 0.0)
    one = jnp.where(lane + sub < 0, 0.0, 1.0)
    cp_q.wait()
    cp_t.wait()

    def store_x(t, q, u, p):
        fx = flux_x(q, u, p)
        for k in range(5):
            eqs[k, t] = EPS * q[k]
            fs[k, t] = (1.0 / 12.0) * fx[k]

    for base in range(0, T, 32):
        def first(t, packs):
            q = [qin[k, pl.ds(t, 8, stride=T), :] for k in range(5)]
            u, v, w, p, c2 = primitive(q)
            rc = lax.rsqrt(c2)
            us[t + 2] = u
            vs[t] = v
            ws[t] = w
            cs[t + 2] = c2 * rc
            rcs[t] = rc
            store_x(t + 2, q, u, p)
            fy = flux_y(q, v, p)
            shift = 2 + 4 * (t - base)
            fresh = []
            for k in range(5):
                f = (1.0 / 12.0) * fy[k]
                e = EPS * q[k]
                f2 = f + f
                r_m2 = pltpu.roll(f + e, 2, 1)
                r_m1 = pltpu.roll(-4.0 * (f2 + e), 1, 1)
                r_p1 = pltpu.roll(4.0 * (f2 - e), 127, 1)
                r_p2 = pltpu.roll(e - f, 126, 1)
                wrap = jnp.where(lane < 1, r_m1, jnp.where(lane > 126, r_p1, 0.0)) + jnp.where(
                    lane < 2, r_m2, jnp.where(lane > 125, r_p2, 0.0)
                )
                total = (r_m2 + r_p2) + (r_m1 + r_p1) + 6.0 * e
                res[k, t] = total - wrap
                fresh.append(packs[k] + pltpu.roll(wrap, shift, 1))
            return tuple(fresh)

        packs = lax.fori_loop(base, min(base + 32, T), first, (zero,) * 5)
        for k in range(5):
            wsend[base // 32, k] = packs[k]

    pl.when(has_u)(w_to_u.start)
    pl.when(has_d)(w_to_d.start)

    pl.when(has_l)(hx_to_r.wait_recv)
    pl.when(has_r)(hx_to_l.wait_recv)

    for t in (-2, -1, T, T + 1):
        q = []
        for k in range(5):
            if t < 0:
                edge = hl[k] if t == -1 else pltpu.roll(hl[k], 1, 0)
                mine = qin[k, pl.ds(T + t, 8, stride=T), :]
                q.append(pltpu.roll(jnp.where(sub == 7, edge, mine), 1, 0))
            else:
                edge = hr[k] if t == T else pltpu.roll(hr[k], 7, 0)
                mine = qin[k, pl.ds(t - T, 8, stride=T), :]
                q.append(pltpu.roll(jnp.where(sub == 0, edge, mine), 7, 0))
        if t < 0:
            outside = jnp.logical_and(sub == 0, ix == 0)
        else:
            outside = jnp.logical_and(sub == 7, ix == nx - 1)
        u, v, w, p, c2 = primitive([jnp.where(outside, 1.0, q[0])] + q[1:])
        us[t + 2] = u
        cs[t + 2] = jnp.sqrt(jnp.where(outside, 1.0, c2))
        store_x(t + 2, q, u, p)

    def matrix_step(t, carry):
        for k in range(5):
            f = [fs[k, t + j] for j in (0, 1, 3, 4)]
            e = [eqs[k, t + j] for j in range(5)]
            x = (
                (f[0] - f[3]) + (e[0] + e[4])
                + (8.0 * (f[2] - f[1]) - 4.0 * (e[1] + e[3])) + 6.0 * e[2]
            )
            res[k, t] = res[k, t] + x
        dt = dtin[pl.ds(t, 8, stride=T), :]
        diag = 8.0 / dt + 6.0
        su = [us[t + 1 + j] for j in range(3)]
        sc = [cs[t + 1 + j] for j in range(3)]
        lu, uu = su[0] + su[1], su[1] + su[2]
        lc, uc = sc[0] + sc[1], sc[1] + sc[2]
        fresh = []
        for m in range(3):
            p1, p2, q1, q2, a1, a2, b1, b2, al0, be0, ah0, bh0, al1, be1, ah1, bh1 = carry[m]
            if m == 0:
                lo, up = lu, uu
            elif m == 1:
                lo, up = lu + lc, uu + uc
            else:
                lo, up = lu - lc, uu - uc
            low = -2.0 * lo - 4.0
            upp = 2.0 * up - 4.0
            rl = low - p2
            piv = (diag - q2) - rl * p1
            inv = 1.0 / piv
            p0 = (upp - rl * q1) * inv
            a0 = -(a2 + rl * a1) * inv
            b0 = -(b2 + rl * b1) * inv
            mat[7 * m + 0, t] = p0
            mat[7 * m + 1, t] = inv
            mat[7 * m + 2, t] = a0
            mat[7 * m + 3, t] = b0
            mat[7 * m + 4, t] = rl
            mat[7 * m + 5, t] = al0
            mat[7 * m + 6, t] = al1
            fresh.append(
                (
                    p0, p1, inv, q1, a0, a1, b0, b1,
                    be0 - al0 * p0, -al0 * inv, ah0 - al0 * a0, bh0 - al0 * b0,
                    be1 - al1 * p0, -al1 * inv, ah1 - al1 * a0, bh1 - al1 * b0,
                )
            )
        return tuple(fresh)

    start = (
        zero, zero, zero, zero, zero, -one, -one, zero,
        -one, zero, zero, zero, zero, -one, zero, zero,
    )
    ends = lax.fori_loop(0, T, matrix_step, (start,) * 3)

    pl.when(has_d)(w_to_u.wait_recv)
    pl.when(has_u)(w_to_d.wait_recv)

    halo_lanes = jnp.logical_or(lane < 2, lane > 125)
    from_up = (lane & 3) < 2
    rhs_carry = ((zero, zero, zero, zero),) * 5
    for base in range(0, T, 32):
        inflow = [jnp.where(from_up, wr[base // 32, k], wl[base // 32, k]) for k in range(5)]

        def rhs_step(t, carry):
            shift = 126 - 4 * (t - base)
            r = []
            for k in range(5):
                got = jnp.where(halo_lanes, pltpu.roll(inflow[k], shift, 1), 0.0)
                r.append(-8.0 * (res[k, t] + got))
            u, v, w, rc = us[t + 2], vs[t], ws[t], rcs[t]
            s = u * u + v * v + w * w
            m = u * r[1] + v * r[2] + w * r[3]
            k2 = (0.4 * rc * rc) * ((0.5 * s) * r[0] - m + r[4])
            kk = 0.5 * k2
            a = (r[1] - u * r[0]) * (0.5 * rc)
            waves = [r[0] - k2, r[2] - v * r[0], r[3] - w * r[0], kk + a, kk - a]
            coef = [[mat[7 * mm_ + j, t] for j in (1, 4, 5, 6)] for mm_ in range(3)]
            fresh = []
            for f in range(5):
                inv, rl, al0, al1 = coef[FAMILY[f]]
                g1, g2, h0, h1 = carry[f]
                g0 = ((waves[f] - g2) - rl * g1) * inv
                gs[f, t] = g0
                fresh.append((g0, g1, h0 - al0 * g0, h1 - al1 * g0))
            return tuple(fresh)

        rhs_carry = lax.fori_loop(base, min(base + 32, T), rhs_step, rhs_carry)

    mats, rhs = [], []
    pieces = []
    for m in range(3):
        p1, p2, q1, q2, a1, a2, b1, b2, al0, be0, ah0, bh0, al1, be1, ah1, bh1 = ends[m]
        pieces.append(p2)
        mats.append(
            (
                (-ah0, -bh0, -ah1, -bh1),
                (-al0, -be0, -al1, -be1),
                (p2 * a1 - a2, p2 * b1 - b2, -a1, -b1),
                (p2 * p1 - q2, p2 * q1, -p1, -q1),
            )
        )
    for f in range(5):
        g1, g2, h0, h1 = rhs_carry[f]
        rhs.append(((h0, h1), (g2 - pieces[FAMILY[f]] * g1, g1)))

    inner = (1, 2, 4)
    mats, rhs, records = reduce_levels(mats, rhs, inner, False)
    flat, tree = jax.tree.flatten((mats, rhs))
    for i, x in enumerate(flat):
        pack[i : i + 1, :] = x[0:1, :]
    mine = pl.ds(pl.multiple_of(ix * ROWS_PACK, 8), ROWS_PACK)
    gathers = [
        remote(pack, gath.at[mine, :], g_send.at[d - 1], g_recv.at[d - 1], (lax.rem(ix + d, nx), iy))
        for d in range(1, nx)
    ]
    for g in gathers:
        g.start()
    own = pltpu.make_async_copy(pack, gath.at[mine, :], in_sem.at[2])
    own.start()
    own.wait()
    for g in gathers:
        g.wait_recv()
    top = [gath[pl.ds(i, 8, stride=ROWS_PACK), :] for i in range(len(flat))]
    t_mats, t_rhs = jax.tree.unflatten(tree, top)
    outer = []
    d = 1
    while d < nx:
        outer.append(d)
        d *= 2
    _, _, t_records = reduce_levels(t_mats, t_rhs, outer, True)
    left, right = expand_levels(t_records, outer, [None] * 5, [None] * 5, sub, True)
    turn = lax.rem(8 - ix, 8)
    left = [tuple(pltpu.roll(x, turn, 0) for x in pair) for pair in left]
    right = [tuple(pltpu.roll(x, turn, 0) for x in pair) for pair in right]
    left, right = expand_levels(records, inner, left, right, sub, False)

    def back_step(i, carry):
        t = T - 1 - i
        coef = [[mat[7 * m + j, t] for j in range(4)] for m in range(3)]
        fresh, x = [], []
        for f in range(5):
            p0, q0, a0, b0 = coef[FAMILY[f]]
            x1, x2 = carry[f]
            l2, l1 = left[f]
            x0 = (gs[f, t] - a0 * l2 - b0 * l1) - p0 * x1 - q0 * x2
            x.append(x0)
            fresh.append((x0, x1))
        u, v, w, c = us[t + 2], vs[t], ws[t], cs[t + 2]
        hs = 0.5 * (u * u + v * v + w * w)
        tt = x[3] + x[4]
        dd = c * (x[3] - x[4])
        base_sum = x[0] + tt
        oo = [
            base_sum,
            u * base_sum + dd,
            v * base_sum + x[1],
            w * base_sum + x[2],
            hs * base_sum + v * x[1] + w * x[2] + 2.5 * (c * c) * tt + u * dd,
        ]
        for k in range(5):
            oout[k, pl.ds(t, 8, stride=T), :] = oo[k]
        return tuple(fresh)

    lax.fori_loop(0, T, back_step, tuple((right[f][0], right[f][1]) for f in range(5)))
    cp_o = pltpu.make_async_copy(oout, out_hbm, out_sem.at[0])
    cp_o.start()
    for g in gathers:
        g.wait_send()
    pl.when(has_r)(hx_to_r.wait_send)
    pl.when(has_l)(hx_to_l.wait_send)
    pl.when(has_u)(w_to_u.wait_send)
    pl.when(has_d)(w_to_d.wait_send)
    cp_o.wait()


def on_device(nx, ny, conserved, time_step):
    rows, cols = conserved.shape[2], conserved.shape[3]
    groups = rows // 8
    blocks = -(-groups // 32)
    f32 = jnp.float32
    vm = lambda *s: pltpu.VMEM(s + (8, 128), f32)
    out = pl.pallas_call(
        functools.partial(kernel, nx, ny, rows),
        out_shape=jax.ShapeDtypeStruct((5, rows, cols), f32),
        in_specs=[pl.BlockSpec(memory_space=pl.ANY)] * 2,
        out_specs=pl.BlockSpec(memory_space=pl.ANY),
        scratch_shapes=[
            pltpu.VMEM((5, rows, cols), f32),
            pltpu.VMEM((rows, cols), f32),
            pltpu.VMEM((5, rows, cols), f32),
            vm(5), vm(5),
            vm(5, groups + 4), vm(5, groups + 4), vm(groups + 4),
            vm(groups), vm(groups), vm(groups + 4), vm(groups),
            vm(5, groups), vm(21, groups), vm(5, groups),
            vm(blocks, 5), vm(blocks, 5), vm(blocks, 5),
            pltpu.VMEM((ROWS_PACK, 128), f32),
            pltpu.VMEM((8 * ROWS_PACK, 128), f32),
            pltpu.SemaphoreType.DMA((3,)),
            pltpu.SemaphoreType.DMA((1,)),
            pltpu.SemaphoreType.DMA((2,)),
            pltpu.SemaphoreType.DMA((2,)),
            pltpu.SemaphoreType.DMA((2,)),
            pltpu.SemaphoreType.DMA((2,)),
            pltpu.SemaphoreType.DMA((max(nx - 1, 1),)),
            pltpu.SemaphoreType.DMA((max(nx - 1, 1),)),
        ],
        compiler_params=pltpu.CompilerParams(
            collective_id=0, has_side_effects=True, vmem_limit_bytes=40 * 1024 * 1024
        ),
    )(conserved.reshape(5, rows, cols), time_step.reshape(rows, cols))
    return out.reshape(conserved.shape)


def solution(mesh):
    return jax.shard_map(
        functools.partial(on_device, mesh.shape["gx"], mesh.shape["gy"]),
        mesh=mesh,
        in_specs=(P(None, None, "gx", "gy"), P(None, "gx", "gy")),
        out_specs=P(None, None, "gx", "gy"),
        check_vma=False,
    )
```

```python
import functools
import jax
import jax.numpy as jnp
from jax import lax
from jax.experimental import pallas as pl
from jax.experimental.pallas import tpu as pltpu
from jax.sharding import PartitionSpec as P

EPS = 0.02
MESH = pl.DeviceIdType.MESH
ROWS_M = 48
ROWS_R = 24
FAMILY = (0, 0, 0, 1, 2)


def primitive(q):
    inv = 1.0 / q[0]
    u = q[1] * inv
    v = q[2] * inv
    w = q[3] * inv
    p = 0.4 * (q[4] - 0.5 * (q[1] * u + q[2] * v + q[3] * w))
    c2 = 1.4 * p * inv
    return u, v, w, p, c2


def flux_x(q, u, p):
    return [q[1], q[1] * u + p, q[2] * u, q[3] * u, (q[4] + p) * u]


def flux_y(q, v, p):
    return [q[2], q[1] * v, q[2] * v + p, q[3] * v, (q[4] + p) * v]


def mm(a, b):
    return (
        a[0] * b[0] + a[1] * b[2],
        a[0] * b[1] + a[1] * b[3],
        a[2] * b[0] + a[3] * b[2],
        a[2] * b[1] + a[3] * b[3],
    )


def mv(a, x):
    return (a[0] * x[0] + a[1] * x[1], a[2] * x[0] + a[3] * x[1])


def add(a, b):
    return tuple(x + y for x, y in zip(a, b))


def schur_inverse(x, y):
    pr = mm(y, x)
    m0, m1, m2, m3 = 1.0 - pr[0], -pr[1], -pr[2], 1.0 - pr[3]
    r = 1.0 / (m0 * m3 - m1 * m2)
    return (m3 * r, -m1 * r, -m2 * r, m0 * r)


def merge_mats(mats_a, mats_b, last):
    mats, rec, invs = [], [], []
    for (hl_a, hr_a, tl_a, tr_a), (hl_b, hr_b, tl_b, tr_b) in zip(mats_a, mats_b):
        minv = schur_inverse(tr_a, hl_b)
        invs.append(minv)
        if last:
            continue
        head_l = mm(minv, mm(hl_b, tl_a))
        head_r = mm(minv, hr_b)
        tail_l = add(tl_a, mm(tr_a, head_l))
        tail_r = mm(tr_a, head_r)
        mats.append(
            (
                add(hl_a, mm(hr_a, head_l)),
                mm(hr_a, head_r),
                mm(tl_b, tail_l),
                add(tr_b, mm(tl_b, tail_r)),
            )
        )
        rec.append((head_l, head_r, tail_l, tail_r))
    return mats, (mats_a, mats_b, invs, rec)


def merge_rhs(level, rhs_a, rhs_b, last):
    mats_a, mats_b, invs, _ = level
    rhs, rec = [], []
    for f, ((h_a, t_a), (h_b, t_b)) in enumerate(zip(rhs_a, rhs_b)):
        m = FAMILY[f]
        head_y = mv(invs[m], add(h_b, mv(mats_b[m][0], t_a)))
        tail_y = add(t_a, mv(mats_a[m][3], head_y))
        rec.append((head_y, tail_y))
        if not last:
            rhs.append((add(h_a, mv(mats_a[m][1], head_y)), add(t_b, mv(mats_b[m][2], tail_y))))
    return rhs, rec


def shifted(tree, d):
    return jax.tree.map(lambda x: pltpu.roll(x, 8 - d, 0), tree)


def reduce_mats(mats, strides, root):
    levels = []
    for d in strides:
        mats, level = merge_mats(mats, shifted(mats, d), root and d == strides[-1])
        levels.append(level)
    return mats, levels


def reduce_rhs(levels, rhs, strides, root):
    records = []
    for level, d in zip(levels, strides):
        rhs, rec = merge_rhs(level, rhs, shifted(rhs, d), root and d == strides[-1])
        records.append((level[3], rec))
    return rhs, records


def expand_levels(records, strides, left, right, sub, root):
    for d, (rec_m, rec_y) in reversed(list(zip(strides, records))):
        upper = (sub & d) != 0
        for f in range(5):
            head, tail = rec_y[f]
            if left[f] is not None:
                hl, hr, tl, tr = rec_m[FAMILY[f]]
                head = add(add(head, mv(hl, left[f])), mv(hr, right[f]))
                tail = add(add(tail, mv(tl, left[f])), mv(tr, right[f]))
                lo, hi = left[f], right[f]
            else:
                lo = hi = (jnp.zeros_like(head[0]),) * 2
            left[f] = tuple(jnp.where(upper, pltpu.roll(x, d, 0), y) for x, y in zip(tail, lo))
            right[f] = tuple(jnp.where(upper, pltpu.roll(y, d, 0), x) for x, y in zip(head, hi))
    return left, right


def kernel(
    nx, ny, rows,
    qin, dtin, oout,
    hl, hr, eqs, fs, us, vs, ws, cs, rcs, res, mat, gs,
    wsend, wl, wr, pack_m, gath_m, pack_r, gath_r,
    in_sem, hx_send, hx_recv, wy_send, wy_recv, gm_send, gm_recv, gr_send, gr_recv,
):
    T = rows // 8
    ix = lax.axis_index("gx")
    iy = lax.axis_index("gy")
    has_l, has_r = ix > 0, ix < nx - 1
    has_d, has_u = iy > 0, iy < ny - 1

    barrier = pltpu.get_barrier_semaphore()
    for d in range(1, nx):
        pl.semaphore_signal(barrier, inc=1, device_id=(lax.rem(ix + d, nx), iy), device_id_type=MESH)

    @pl.when(has_d)
    def _():
        pl.semaphore_signal(barrier, inc=1, device_id=(ix, iy - 1), device_id_type=MESH)

    @pl.when(has_u)
    def _():
        pl.semaphore_signal(barrier, inc=1, device_id=(ix, iy + 1), device_id_type=MESH)

    def remote(src, dst, s_sem, r_sem, target):
        return pltpu.make_async_remote_copy(
            src_ref=src, dst_ref=dst, send_sem=s_sem, recv_sem=r_sem,
            device_id=target, device_id_type=MESH,
        )

    right_x = (lax.rem(ix + 1, nx), iy)
    left_x = (lax.rem(ix + nx - 1, nx), iy)
    up_y = (ix, lax.rem(iy + 1, ny))
    down_y = (ix, lax.rem(iy + ny - 1, ny))
    hx_to_r = remote(qin.at[:, pl.ds(rows - 8, 8), :], hl, hx_send.at[0], hx_recv.at[0], right_x)
    hx_to_l = remote(qin.at[:, pl.ds(0, 8), :], hr, hx_send.at[1], hx_recv.at[1], left_x)
    w_to_u = remote(wsend, wl, wy_send.at[0], wy_recv.at[0], up_y)
    w_to_d = remote(wsend, wr, wy_send.at[1], wy_recv.at[1], down_y)

    if ny > 1:
        both = jnp.logical_and(has_d, has_u)

        @pl.when(both)
        def _():
            pl.semaphore_wait(barrier, nx + 1)

        @pl.when(jnp.logical_not(both))
        def _():
            pl.semaphore_wait(barrier, nx)
    else:
        pl.semaphore_wait(barrier, nx - 1)

    pl.when(has_r)(hx_to_r.start)
    pl.when(has_l)(hx_to_l.start)

    @pl.when(jnp.logical_not(has_l))
    def _():
        hl[...] = jnp.zeros_like(hl)

    @pl.when(jnp.logical_not(has_r))
    def _():
        hr[...] = jnp.zeros_like(hr)

    @pl.when(jnp.logical_not(has_d))
    def _():
        wl[...] = jnp.zeros_like(wl)

    @pl.when(jnp.logical_not(has_u))
    def _():
        wr[...] = jnp.zeros_like(wr)

    if nx < 8:
        for gath, n in ((gath_m, ROWS_M), (gath_r, ROWS_R)):
            gath[pl.ds(nx * n, (8 - nx) * n), :] = jnp.zeros(((8 - nx) * n, 128), jnp.float32)

    pack_r[16:24, :] = jnp.zeros((8, 128), jnp.float32)
    shape = (8, 128)
    lane = lax.broadcasted_iota(jnp.int32, shape, 1)
    sub = lax.broadcasted_iota(jnp.int32, shape, 0)
    zero = jnp.where(lane + sub < 0, 1.0, 0.0)
    one = jnp.where(lane + sub < 0, 0.0, 1.0)

    def store_x(t, q, u, p):
        fx = flux_x(q, u, p)
        for k in range(5):
            eqs[k, t] = EPS * q[k]
            fs[k, t] = (1.0 / 12.0) * fx[k]

    for base in range(0, T, 32):
        def first(t, packs):
            q = [qin[k, pl.ds(t, 8, stride=T), :] for k in range(5)]
            u, v, w, p, c2 = primitive(q)
            rc = lax.rsqrt(c2)
            us[t + 2] = u
            vs[t] = v
            ws[t] = w
            cs[t + 2] = c2 * rc
            rcs[t] = rc
            store_x(t + 2, q, u, p)
            fy = flux_y(q, v, p)
            shift = 2 + 4 * (t - base)
            fresh = []
            for k in range(5):
                f = (1.0 / 12.0) * fy[k]
                e = EPS * q[k]
                f2 = f + f
                r_m2 = pltpu.roll(f + e, 2, 1)
                r_m1 = pltpu.roll(-4.0 * (f2 + e), 1, 1)
                r_p1 = pltpu.roll(4.0 * (f2 - e), 127, 1)
                r_p2 = pltpu.roll(e - f, 126, 1)
                wrap = jnp.where(lane < 1, r_m1, jnp.where(lane > 126, r_p1, 0.0)) + jnp.where(
                    lane < 2, r_m2, jnp.where(lane > 125, r_p2, 0.0)
                )
                total = (r_m2 + r_p2) + (r_m1 + r_p1) + 6.0 * e
                res[k, t] = total - wrap
                fresh.append(packs[k] + pltpu.roll(wrap, shift, 1))
            return tuple(fresh)

        packs = lax.fori_loop(base, min(base + 32, T), first, (zero,) * 5, unroll=4)
        for k in range(5):
            wsend[base // 32, k] = packs[k]

    pl.when(has_u)(w_to_u.start)
    pl.when(has_d)(w_to_d.start)

    pl.when(has_l)(hx_to_r.wait_recv)
    pl.when(has_r)(hx_to_l.wait_recv)

    for t in (-2, -1, T, T + 1):
        q = []
        for k in range(5):
            if t < 0:
                edge = hl[k] if t == -1 else pltpu.roll(hl[k], 1, 0)
                mine = qin[k, pl.ds(T + t, 8, stride=T), :]
                q.append(pltpu.roll(jnp.where(sub == 7, edge, mine), 1, 0))
            else:
                edge = hr[k] if t == T else pltpu.roll(hr[k], 7, 0)
                mine = qin[k, pl.ds(t - T, 8, stride=T), :]
                q.append(pltpu.roll(jnp.where(sub == 0, edge, mine), 7, 0))
        if t < 0:
            outside = jnp.logical_and(sub == 0, ix == 0)
        else:
            outside = jnp.logical_and(sub == 7, ix == nx - 1)
        u, v, w, p, c2 = primitive([jnp.where(outside, 1.0, q[0])] + q[1:])
        us[t + 2] = u
        cs[t + 2] = jnp.sqrt(jnp.where(outside, 1.0, c2))
        store_x(t + 2, q, u, p)

    def matrix_step(t, carry):
        for k in range(5):
            f = [fs[k, t + j] for j in (0, 1, 3, 4)]
            e = [eqs[k, t + j] for j in range(5)]
            x = (
                (f[0] - f[3]) + (e[0] + e[4])
                + (8.0 * (f[2] - f[1]) - 4.0 * (e[1] + e[3])) + 6.0 * e[2]
            )
            res[k, t] = res[k, t] + x
        dt = dtin[pl.ds(t, 8, stride=T), :]
        diag = 8.0 / dt + 6.0
        su = [us[t + 1 + j] for j in range(3)]
        sc = [cs[t + 1 + j] for j in range(3)]
        lu, uu = su[0] + su[1], su[1] + su[2]
        lc, uc = sc[0] + sc[1], sc[1] + sc[2]
        fresh = []
        for m in range(3):
            p1, p2, q1, q2, a1, a2, b1, b2, al0, be0, ah0, bh0, al1, be1, ah1, bh1 = carry[m]
            if m == 0:
                lo, up = lu, uu
            elif m == 1:
                lo, up = lu + lc, uu + uc
            else:
                lo, up = lu - lc, uu - uc
            low = -2.0 * lo - 4.0
            upp = 2.0 * up - 4.0
            rl = low - p2
            piv = (diag - q2) - rl * p1
            inv = 1.0 / piv
            p0 = (upp - rl * q1) * inv
            a0 = -(a2 + rl * a1) * inv
            b0 = -(b2 + rl * b1) * inv
            mat[7 * m + 0, t] = p0
            mat[7 * m + 1, t] = inv
            mat[7 * m + 2, t] = a0
            mat[7 * m + 3, t] = b0
            mat[7 * m + 4, t] = rl
            mat[7 * m + 5, t] = al0
            mat[7 * m + 6, t] = al1
            fresh.append(
                (
                    p0, p1, inv, q1, a0, a1, b0, b1,
                    be0 - al0 * p0, -al0 * inv, ah0 - al0 * a0, bh0 - al0 * b0,
                    be1 - al1 * p0, -al1 * inv, ah1 - al1 * a0, bh1 - al1 * b0,
                )
            )
        return tuple(fresh)

    start = (
        zero, zero, zero, zero, zero, -one, -one, zero,
        -one, zero, zero, zero, zero, -one, zero, zero,
    )
    ends = lax.fori_loop(0, T, matrix_step, (start,) * 3, unroll=4)

    mats = []
    pieces = []
    for m in range(3):
        p1, p2, q1, q2, a1, a2, b1, b2, al0, be0, ah0, bh0, al1, be1, ah1, bh1 = ends[m]
        pieces.append(p2)
        mats.append(
            (
                (-ah0, -bh0, -ah1, -bh1),
                (-al0, -be0, -al1, -be1),
                (p2 * a1 - a2, p2 * b1 - b2, -a1, -b1),
                (p2 * p1 - q2, p2 * q1, -p1, -q1),
            )
        )
    inner = (1, 2, 4)
    outer = []
    d = 1
    while d < nx:
        outer.append(d)
        d *= 2
    mats, levels = reduce_mats(mats, inner, False)

    def exchange(tree, pack, gath, n_rows, g_send, g_recv, own_sem):
        flat, form = jax.tree.flatten(tree)
        for i, x in enumerate(flat):
            pack[i : i + 1, :] = x[0:1, :]
        mine = gath.at[pl.ds(pl.multiple_of(ix * n_rows, 8), n_rows), :]
        copies = [
            remote(pack, mine, g_send.at[d - 1], g_recv.at[d - 1], (lax.rem(ix + d, nx), iy))
            for d in range(1, nx)
        ]
        for g in copies:
            g.start()
        own = pltpu.make_async_copy(pack, mine, own_sem)
        own.start()

        def finish():
            own.wait()
            for g in copies:
                g.wait_recv()
            top = [gath[pl.ds(i, 8, stride=n_rows), :] for i in range(len(flat))]
            return jax.tree.unflatten(form, top)

        return copies, finish

    copies_m, finish_m = exchange(mats, pack_m, gath_m, ROWS_M, gm_send, gm_recv, in_sem.at[0])

    pl.when(has_d)(w_to_u.wait_recv)
    pl.when(has_u)(w_to_d.wait_recv)

    halo_lanes = jnp.logical_or(lane < 2, lane > 125)
    from_up = (lane & 3) < 2
    rhs_carry = ((zero, zero, zero, zero),) * 5
    for base in range(0, T, 32):
        inflow = [jnp.where(from_up, wr[base // 32, k], wl[base // 32, k]) for k in range(5)]

        def rhs_step(t, carry):
            shift = 126 - 4 * (t - base)
            r = []
            for k in range(5):
                got = jnp.where(halo_lanes, pltpu.roll(inflow[k], shift, 1), 0.0)
                r.append(-8.0 * (res[k, t] + got))
            u, v, w, rc = us[t + 2], vs[t], ws[t], rcs[t]
            s = u * u + v * v + w * w
            m = u * r[1] + v * r[2] + w * r[3]
            k2 = (0.4 * rc * rc) * ((0.5 * s) * r[0] - m + r[4])
            kk = 0.5 * k2
            a = (r[1] - u * r[0]) * (0.5 * rc)
            waves = [r[0] - k2, r[2] - v * r[0], r[3] - w * r[0], kk + a, kk - a]
            coef = [[mat[7 * mm_ + j, t] for j in (1, 4, 5, 6)] for mm_ in range(3)]
            fresh = []
            for f in range(5):
                inv, rl, al0, al1 = coef[FAMILY[f]]
                g1, g2, h0, h1 = carry[f]
                g0 = ((waves[f] - g2) - rl * g1) * inv
                gs[f, t] = g0
                fresh.append((g0, g1, h0 - al0 * g0, h1 - al1 * g0))
            return tuple(fresh)

        rhs_carry = lax.fori_loop(base, min(base + 32, T), rhs_step, rhs_carry, unroll=8)

    rhs = []
    for f in range(5):
        g1, g2, h0, h1 = rhs_carry[f]
        rhs.append(((h0, h1), (g2 - pieces[FAMILY[f]] * g1, g1)))

    rhs, records = reduce_rhs(levels, rhs, inner, False)
    copies_r, finish_r = exchange(rhs, pack_r, gath_r, ROWS_R, gr_send, gr_recv, in_sem.at[1])
    _, t_levels = reduce_mats(finish_m(), outer, True)
    _, t_records = reduce_rhs(t_levels, finish_r(), outer, True)
    left, right = expand_levels(t_records, outer, [None] * 5, [None] * 5, sub, True)
    turn = lax.rem(8 - ix, 8)
    left = [tuple(pltpu.roll(x, turn, 0) for x in pair) for pair in left]
    right = [tuple(pltpu.roll(x, turn, 0) for x in pair) for pair in right]
    left, right = expand_levels(records, inner, left, right, sub, False)

    def back_step(i, carry):
        t = T - 1 - i
        coef = [[mat[7 * m + j, t] for j in range(4)] for m in range(3)]
        fresh, x = [], []
        for f in range(5):
            p0, q0, a0, b0 = coef[FAMILY[f]]
            x1, x2 = carry[f]
            l2, l1 = left[f]
            x0 = (gs[f, t] - a0 * l2 - b0 * l1) - p0 * x1 - q0 * x2
            x.append(x0)
            fresh.append((x0, x1))
        u, v, w, c = us[t + 2], vs[t], ws[t], cs[t + 2]
        hs = 0.5 * (u * u + v * v + w * w)
        tt = x[3] + x[4]
        dd = c * (x[3] - x[4])
        base_sum = x[0] + tt
        oo = [
            base_sum,
            u * base_sum + dd,
            v * base_sum + x[1],
            w * base_sum + x[2],
            hs * base_sum + v * x[1] + w * x[2] + 2.5 * (c * c) * tt + u * dd,
        ]
        for k in range(5):
            oout[k, pl.ds(t, 8, stride=T), :] = oo[k]
        return tuple(fresh)

    lax.fori_loop(0, T, back_step, tuple((right[f][0], right[f][1]) for f in range(5)), unroll=4)
    for g in copies_m + copies_r:
        g.wait_send()
    pl.when(has_r)(hx_to_r.wait_send)
    pl.when(has_l)(hx_to_l.wait_send)
    pl.when(has_u)(w_to_u.wait_send)
    pl.when(has_d)(w_to_d.wait_send)


def on_device(nx, ny, conserved, time_step):
    rows, cols = conserved.shape[2], conserved.shape[3]
    groups = rows // 8
    blocks = -(-groups // 32)
    f32 = jnp.float32
    vm = lambda *s: pltpu.VMEM(s + (8, 128), f32)
    out = pl.pallas_call(
        functools.partial(kernel, nx, ny, rows),
        out_shape=jax.ShapeDtypeStruct((5, rows, cols), f32),
        in_specs=[pl.BlockSpec(memory_space=pltpu.VMEM)] * 2,
        out_specs=pl.BlockSpec(memory_space=pltpu.VMEM),
        scratch_shapes=[
            vm(5), vm(5),
            vm(5, groups + 4), vm(5, groups + 4), vm(groups + 4),
            vm(groups), vm(groups), vm(groups + 4), vm(groups),
            vm(5, groups), vm(21, groups), vm(5, groups),
            vm(blocks, 5), vm(blocks, 5), vm(blocks, 5),
            pltpu.VMEM((ROWS_M, 128), f32),
            pltpu.VMEM((8 * ROWS_M, 128), f32),
            pltpu.VMEM((ROWS_R, 128), f32),
            pltpu.VMEM((8 * ROWS_R, 128), f32),
            pltpu.SemaphoreType.DMA((2,)),
            pltpu.SemaphoreType.DMA((2,)),
            pltpu.SemaphoreType.DMA((2,)),
            pltpu.SemaphoreType.DMA((2,)),
            pltpu.SemaphoreType.DMA((2,)),
            pltpu.SemaphoreType.DMA((max(nx - 1, 1),)),
            pltpu.SemaphoreType.DMA((max(nx - 1, 1),)),
            pltpu.SemaphoreType.DMA((max(nx - 1, 1),)),
            pltpu.SemaphoreType.DMA((max(nx - 1, 1),)),
        ],
        compiler_params=pltpu.CompilerParams(
            collective_id=0, has_side_effects=True, vmem_limit_bytes=40 * 1024 * 1024
        ),
    )(conserved.reshape(5, rows, cols), time_step.reshape(rows, cols))
    return out.reshape(conserved.shape)


def solution(mesh):
    return jax.shard_map(
        functools.partial(on_device, mesh.shape["gx"], mesh.shape["gy"]),
        mesh=mesh,
        in_specs=(P(None, None, "gx", "gy"), P(None, "gx", "gy")),
        out_specs=P(None, None, "gx", "gy"),
        check_vma=False,
    )
```
